512 devices in a mesh: row: 16 (over x, y), col: 16 (over z), layer: 2 (over core).
Axes of the slice: x: 4, y: 4, z: 16, core: 2. Of those that a mesh axis runs over, the one named last changes fastest.
Arguments:
- density: bfloat16 [6144, 6144], P('row', 'col'), may hold values from -1 to 1.5, as said below
- product_pattern: int32 [96, 96], P('row', 'col'), may hold values from 0 to 1, as said below
Outputs:
- purified: bfloat16 [6144, 6144], P(('row', 'layer'), 'col')
The draws below stay inside these ranges and needn't reach their ends.
Inputs may be any that keep to these rules, and one draw needn't show every extreme that they name: `density`: symmetric; zero outside a symmetric pattern of 64 x 64 tiles that holds every diagonal tile. `product_pattern`: 0 or 1; symmetric; every diagonal tile is 1.
All inputs are finite; a program needn't handle non-finite values.
Results may differ from the reference program's by a relative error of at most 0.006.
Values may be sent and summed in bfloat16 or wider, within the bound.
No kernel may reach another device: no remote copies, remote signals or barrier semaphores. Data moves between devices by JAX's collectives and lax.ppermute only.
A program may use at most 64 MiB of HBM per device.

```python
import math
import jax
import jax.numpy as jnp

TILE = 64
NTILES = 96
ORDER = 6144


def tile_pattern(key, tile_count, floor_level, slope):
    row_ids = jnp.arange(tile_count, dtype=jnp.int32)[:, None]
    col_ids = jnp.arange(tile_count, dtype=jnp.int32)[None, :]
    distance = jnp.abs(row_ids - col_ids)
    threshold = jnp.maximum(floor_level, 100 - slope * distance)
    threshold = jnp.where(distance == 0, 101, threshold)
    rolled = jax.random.randint(key, (tile_count, tile_count), 0, 100, dtype=jnp.int32)
    mirrored = jnp.where(row_ids <= col_ids, rolled, rolled.T)
    return (mirrored < threshold).astype(jnp.int32)


def draw_density(key, part):
    key = jax.random.fold_in(key, 11)
    key_mask, key_values = jax.random.split(key, 2)
    tile_mask = tile_pattern(key_mask, NTILES, 12, 9)
    tile_grid = tile_mask.astype(jnp.float32)[:, None, :, None]
    element_mask = jnp.broadcast_to(tile_grid, (NTILES, TILE, NTILES, TILE)).reshape(ORDER, ORDER)
    spread = 0.5 / math.sqrt(TILE * min(NTILES, 24))
    raw_values = jax.random.normal(key_values, (ORDER, ORDER), jnp.float32)
    row_ids = jnp.arange(ORDER, dtype=jnp.int32)[:, None]
    col_ids = jnp.arange(ORDER, dtype=jnp.int32)[None, :]
    mirrored = jnp.where(row_ids <= col_ids, raw_values, raw_values.T)
    result = mirrored * spread * element_mask + 0.3 * (row_ids == col_ids).astype(jnp.float32)
    return result.astype(jnp.bfloat16)


def draw_product_pattern(key, part):
    key = jax.random.fold_in(key, 23)
    return tile_pattern(key, NTILES, 25, 6)


def setup_inputs(seed: int = 0) -> dict:
    key_of = jax.random.split(jax.random.key(seed), 3)
    density = draw_density(jax.random.fold_in(key_of[2], 71), 0)
    product_pattern = draw_product_pattern(jax.random.fold_in(key_of[2], 71), 0)
    return {"density": density, "product_pattern": product_pattern}


def expand_tiles(tile_mask):
    tile_rows, tile_cols = tile_mask.shape
    tile_grid = tile_mask.astype(jnp.float32)[:, None, :, None]
    return jnp.broadcast_to(tile_grid, (tile_rows, TILE, tile_cols, TILE)).reshape(tile_rows * TILE, tile_cols * TILE)


def reference(density, product_pattern):
    element_mask = expand_tiles(product_pattern)
    full_square = jnp.dot(density, density, preferred_element_type=jnp.float32)
    squared = (full_square * element_mask).astype(jnp.bfloat16)
    cubed_term = jnp.dot(squared, density, preferred_element_type=jnp.float32)
    return ((3.0 * squared.astype(jnp.float32) - 2.0 * cubed_term) * element_mask).astype(jnp.bfloat16)
```

```python
import jax
import jax.numpy as jnp
from jax import lax
from jax.sharding import PartitionSpec as P

TILE = 64


def expand_tiles(tile_mask):
    tile_rows, tile_cols = tile_mask.shape
    tile_grid = tile_mask.astype(jnp.float32)[:, None, :, None]
    return jnp.broadcast_to(tile_grid, (tile_rows, TILE, tile_cols, TILE)).reshape(
        tile_rows * TILE, tile_cols * TILE
    )


def strip_product(left_blocks, right_blocks):
    total = jnp.dot(left_blocks[0], right_blocks[0], preferred_element_type=jnp.float32)
    for k in range(1, left_blocks.shape[0]):
        total += jnp.dot(left_blocks[k], right_blocks[k], preferred_element_type=jnp.float32)
    return total


def shards(density, product_pattern):
    layers = lax.axis_size("layer")
    layer_pos = lax.axis_index("layer")
    half_rows = density.shape[0] // layers
    mask_rows = lax.dynamic_slice_in_dim(
        product_pattern, layer_pos * (half_rows // TILE), half_rows // TILE, 0
    )
    mask = expand_tiles(mask_rows)
    mine = lax.dynamic_slice_in_dim(density, layer_pos * half_rows, half_rows, 0)
    left = lax.all_gather(mine, "col")
    right = lax.all_gather(density, "row")
    squared = (strip_product(left, right) * mask).astype(jnp.bfloat16)
    left = lax.all_gather(squared, "col")
    cubed = strip_product(left, right)
    result = (3.0 * squared.astype(jnp.float32) - 2.0 * cubed) * mask
    return result.astype(jnp.bfloat16)


def solution(mesh):
    placed = (P("row", "col"), P("row", "col"))
    return jax.shard_map(
        shards, mesh=mesh, in_specs=placed, out_specs=P(("row", "layer"), "col"), check_vma=False
    )
```

```python
import jax
import jax.numpy as jnp
from jax import lax
from jax.sharding import PartitionSpec as P

TILE = 64
TAIL = 8


def expand_tiles(tile_mask):
    tile_rows, tile_cols = tile_mask.shape
    tile_grid = tile_mask.astype(jnp.float32)[:, None, :, None]
    return jnp.broadcast_to(tile_grid, (tile_rows, TILE, tile_cols, TILE)).reshape(
        tile_rows * TILE, tile_cols * TILE
    )


def pack(block):
    block = block.astype(jnp.float32)
    largest = jnp.maximum(jnp.max(jnp.abs(block)), 1e-30)
    exponent = jnp.floor(jnp.log2(largest))
    scaled = (block * jnp.exp2(14.0 - exponent)).astype(jnp.float16)
    tail = jnp.full((TAIL, block.shape[1]), exponent).astype(jnp.float16)
    return jnp.concatenate([scaled, tail])


def unpack(packed):
    exponent = packed[:, -TAIL:-TAIL + 1, :1].astype(jnp.float32)
    return (packed[:, :-TAIL].astype(jnp.float32) * jnp.exp2(exponent - 14.0)).astype(jnp.bfloat16)


def shards(density, product_pattern):
    layers = lax.axis_size("layer")
    layer_pos = lax.axis_index("layer")
    rows = lax.axis_size("row")
    cols = lax.axis_size("col")
    side = density.shape[0]
    half = side // layers

    mine = lax.dynamic_slice_in_dim(density, layer_pos * half, half, 0)
    mine_t = lax.dynamic_slice_in_dim(density.T, layer_pos * half, half, 0)
    right = lax.all_to_all(jnp.broadcast_to(mine_t, (rows, half, side)), "row", 0, 0)
    left = lax.all_gather(pack(mine), ("col", "layer"))
    left = unpack(left).reshape(cols, side, side)
    other = lax.ppermute(right, "layer", [(i, layers - 1 - i) for i in range(layers)])

    mask = expand_tiles(product_pattern)
    mask_t = lax.dynamic_slice_in_dim(mask.T, layer_pos * half, half, 0)
    total = jnp.einsum("kjc,krc->jr", right, left, preferred_element_type=jnp.float32)
    squared_t = (total * mask_t).astype(jnp.bfloat16)
    strip = unpack(lax.all_gather(pack(squared_t), ("col", "layer"))).reshape(cols * side, side)
    strip = lax.dynamic_slice_in_dim(strip, layer_pos * half, half, 1).reshape(cols, side, half)

    low = jnp.where(layer_pos == 0, right, other)
    high = jnp.where(layer_pos == 0, other, right)
    cubed_t = jnp.concatenate(
        [
            jnp.einsum("kjc,kcr->jr", part, strip, preferred_element_type=jnp.float32)
            for part in (low, high)
        ]
    )
    square_t = lax.dynamic_index_in_dim(strip, lax.axis_index("col"), 0, keepdims=False)
    mask_rows = lax.dynamic_slice_in_dim(mask, layer_pos * half, half, 0)
    result = (3.0 * square_t.astype(jnp.float32) - 2.0 * cubed_t).T * mask_rows
    return result.astype(jnp.bfloat16)


def solution(mesh):
    placed = (P("row", "col"), P("row", "col"))
    return jax.shard_map(
        shards, mesh=mesh, in_specs=placed, out_specs=P(("row", "layer"), "col"), check_vma=False
    )
```

```python
import functools

import jax
import jax.numpy as jnp
from jax import lax
from jax.experimental import pallas as pl
from jax.experimental.pallas import tpu as pltpu
from jax.sharding import PartitionSpec as P

TILE = 64
TOP = 32767.0
POWER = 17
F32, BF16 = jnp.float32, jnp.bfloat16


def encode(values, bound):
    size = jnp.abs(values) * (1.0 / bound)
    level = jnp.exp(jnp.log(jnp.maximum(size, 1e-37)) * (1.0 / POWER)) * TOP + 0.5
    level = jnp.where(size > 1e-36, jnp.minimum(level, TOP), 0.0)
    return jnp.where(values < 0, -level, level).astype(jnp.int32).astype(jnp.int16)


def decode(codes, bound):
    q = codes.astype(jnp.int32).astype(F32)
    s = q * (1.0 / TOP)
    s2 = s * s
    s4 = s2 * s2
    s8 = s4 * s4
    return ((s8 * s8) * (s * bound)).astype(BF16)


def masked_rows(pattern_ref, first, count, columns, transposed):
    lane_tile = lax.broadcasted_iota(jnp.int32, (TILE, columns), 1) // TILE
    out = []
    for i in range(count):
        row = jnp.zeros((TILE, columns), F32)
        for j in range(columns // TILE):
            here = pattern_ref[j, first + i] if transposed else pattern_ref[first + i, j]
            row = jnp.where(lane_tile == j, here.astype(F32), row)
        out.append(row)
    return jnp.concatenate(out, axis=0)


def start_kernel(layer_ref, block_ref, copies_ref, code_ref, turned, *, bound):
    half = code_ref.shape[0]
    turned[...] = block_ref[...].astype(F32).T
    first = pl.multiple_of(layer_ref[0] * half, half)
    mine = turned[pl.ds(first, half), :]
    code_ref[...] = encode(mine, bound)
    for i in range(copies_ref.shape[0]):
        copies_ref[i] = mine.astype(BF16)


def square_kernel(layer_ref, pattern_ref, right_ref, left_ref, code_ref, *, pair, bounds):
    blocks, half, side = right_ref.shape
    total = jnp.zeros((half, side), F32)
    for k in range(0, blocks, pair):
        right = jnp.concatenate([right_ref[k + i] for i in range(pair)], axis=1)
        left = decode(left_ref[k * side : (k + pair) * side, :], bounds[0])
        total += jnp.dot(right, left, preferred_element_type=F32)
    tiles = half // TILE
    mask = masked_rows(pattern_ref, layer_ref[0] * tiles, tiles, side, True)
    squared = (total * mask).astype(BF16).astype(F32)
    code_ref[...] = encode(squared, bounds[1])


def cube_kernel(
    place_ref, pattern_ref, own_ref, other_ref, strip_ref, out_ref, joined, turned, *, pair, bound
):
    layer, col = place_ref[0], place_ref[1]
    blocks, half, side = own_ref.shape
    width = joined.shape[1]
    lanes = pl.ds(pl.multiple_of(layer * (side - width), 128), width)
    totals = [jnp.zeros((half, width), F32), jnp.zeros((half, width), F32)]
    for k in range(0, blocks, pair):
        strip = decode(strip_ref[k * side : (k + pair) * side, lanes], bound)
        for n, ref in enumerate((own_ref, other_ref)):
            right = jnp.concatenate([ref[k + i] for i in range(pair)], axis=1)
            totals[n] += jnp.dot(right, strip, preferred_element_type=F32)
    joined[pl.ds(pl.multiple_of(layer * half, half), half), :] = totals[0]
    joined[pl.ds(pl.multiple_of((1 - layer) * half, half), half), :] = totals[1]
    square = decode(strip_ref[pl.ds(pl.multiple_of(col * side, side), side), lanes], bound)
    turned[...] = (3.0 * square.astype(F32) - 2.0 * joined[...]).T
    skip = side - half - (side - width)
    rows = turned[pl.ds(pl.multiple_of(layer * skip, 8), half), :]
    tiles = half // TILE
    mask = masked_rows(pattern_ref, layer * tiles, tiles, side, False)
    out_ref[...] = (rows * mask).astype(BF16)


def shards(density, product_pattern):
    layers = lax.axis_size("layer")
    layer_pos = lax.axis_index("layer")
    rows, cols = lax.axis_size("row"), lax.axis_size("col")
    side = density.shape[0]
    half = side // layers
    bound = 2.0
    square_bound = 2.0 ** (2 + (side * rows - 1).bit_length() - 1)
    vmem = pl.BlockSpec(memory_space=pltpu.VMEM)
    smem = pl.BlockSpec(memory_space=pltpu.SMEM)
    params = pltpu.CompilerParams(vmem_limit_bytes=56 * 1024 * 1024)
    layer = jnp.reshape(layer_pos, (1,)).astype(jnp.int32)
    place = jnp.stack([layer_pos, lax.axis_index("col")]).astype(jnp.int32)

    copies, code = pl.pallas_call(
        functools.partial(start_kernel, bound=bound),
        out_shape=(
            jax.ShapeDtypeStruct((rows, half, side), BF16),
            jax.ShapeDtypeStruct((half, side), jnp.int16),
        ),
        in_specs=[smem, vmem],
        out_specs=(vmem, vmem),
        scratch_shapes=[pltpu.VMEM((side, side), F32)],
        compiler_params=params,
    )(layer, density)
    right = lax.all_to_all(copies, "row", 0, 0)
    left = lax.all_gather(code, ("col", "layer"), tiled=True)
    code = pl.pallas_call(
        functools.partial(square_kernel, pair=2, bounds=(bound, square_bound)),
        out_shape=jax.ShapeDtypeStruct((half, side), jnp.int16),
        in_specs=[smem, smem, vmem, vmem],
        out_specs=vmem,
        compiler_params=params,
    )(layer, product_pattern, right, left)
    other = lax.ppermute(right, "layer", [(i, layers - 1 - i) for i in range(layers)])
    strip = lax.all_gather(code, ("col", "layer"), tiled=True)
    width = -(-half // 128) * 128
    return pl.pallas_call(
        functools.partial(cube_kernel, pair=2, bound=square_bound),
        out_shape=jax.ShapeDtypeStruct((half, side), BF16),
        in_specs=[smem, smem, vmem, vmem, vmem],
        out_specs=vmem,
        scratch_shapes=[pltpu.VMEM((side, width), F32), pltpu.VMEM((width, side), F32)],
        compiler_params=params,
    )(place, product_pattern, right, other, strip)


def solution(mesh):
    placed = (P("row", "col"), P("row", "col"))
    return jax.shard_map(
        shards, mesh=mesh, in_specs=placed, out_specs=P(("row", "layer"), "col"), check_vma=False
    )
```

```python
import functools

import jax
import jax.numpy as jnp
from jax import lax
from jax.experimental import pallas as pl
from jax.experimental.pallas import tpu as pltpu
from jax.sharding import PartitionSpec as P

TILE = 64
STEP = 2.0**-15
POWER = 17
F32, BF16 = jnp.float32, jnp.bfloat16


def encode(values, bound):
    size = jnp.abs(values) * (1.0 / bound)
    level = jnp.exp(jnp.log(jnp.maximum(size, 1e-37)) * (1.0 / POWER)) * (1.0 / STEP) + 0.5
    level = jnp.where(size > 1e-36, jnp.minimum(level, 32767.0), 0.0)
    return jnp.where(values < 0, -level, level).astype(jnp.int32).astype(jnp.int16)


def decode(codes):
    q = codes.astype(jnp.int32).astype(F32)
    s2 = (q * q) * (STEP * STEP)
    s4 = s2 * s2
    s8 = s4 * s4
    return ((s8 * s8) * q).astype(BF16)


def fetch(source, chunks, sems):
    rows = chunks.shape[1]
    copies = [
        pltpu.make_async_copy(source.at[pl.ds(n * rows, rows)], chunks.at[n], sems.at[n])
        for n in range(chunks.shape[0])
    ]
    for copy in copies:
        copy.start()
    return copies


def masked_rows(pattern_ref, first, count, columns, transposed):
    lane_tile = lax.broadcasted_iota(jnp.int32, (TILE, columns), 1) // TILE
    out = []
    for i in range(count):
        row = jnp.zeros((TILE, columns), F32)
        for j in range(columns // TILE):
            here = pattern_ref[j, first + i] if transposed else pattern_ref[first + i, j]
            row = jnp.where(lane_tile == j, here.astype(F32), row)
        out.append(row)
    return jnp.concatenate(out, axis=0)


def start_kernel(layer_ref, block_ref, copies_ref, code_ref, turned, mine, sems, *, bound):
    half = code_ref.shape[0]
    turned[...] = block_ref[...].astype(F32).T
    values = turned[pl.ds(pl.multiple_of(layer_ref[0] * half, half), half), :]
    mine[...] = values.astype(BF16)
    copies = [
        pltpu.make_async_copy(mine, copies_ref.at[n], sems.at[n])
        for n in range(copies_ref.shape[0])
    ]
    for copy in copies:
        copy.start()
    code_ref[...] = encode(values, bound)
    for copy in copies:
        copy.wait()


def square_kernel(
    layer_ref,
    pattern_ref,
    right_ref,
    left_ref,
    code_ref,
    right_chunks,
    left_chunks,
    right_sems,
    left_sems,
    *,
    pair,
    bounds,
):
    half, side = code_ref.shape
    rights = fetch(right_ref, right_chunks, right_sems)
    lefts = fetch(left_ref, left_chunks, left_sems)
    tiles = half // TILE
    mask = masked_rows(pattern_ref, layer_ref[0] * tiles, tiles, side, True)
    total = jnp.zeros((half, side), F32)
    for n in range(len(lefts)):
        lefts[n].wait()
        left = decode(left_chunks[n])
        rights[n].wait()
        right = jnp.concatenate([right_chunks[n, i] for i in range(pair)], axis=1)
        total += jnp.dot(right, left, preferred_element_type=F32)
    squared = (total * (bounds[0] * STEP) * mask).astype(BF16).astype(F32)
    code_ref[...] = encode(squared, bounds[1])


def cube_kernel(
    layer_ref,
    col_ref,
    pattern_ref,
    own_ref,
    other_ref,
    strip_ref,
    out_ref,
    joined,
    turned,
    chunks,
    sems,
    *,
    pair,
    bound,
):
    layer = layer_ref[0]
    blocks, half, side = own_ref.shape
    copies = fetch(other_ref, chunks, sems)
    rows = pair * side
    width = joined.shape[1]
    lanes = pl.ds(pl.multiple_of(layer * (side - width), 128), width)
    totals = [jnp.zeros((half, width), F32), jnp.zeros((half, width), F32)]
    for n in range(blocks // pair):
        strip = decode(strip_ref[n * rows : (n + 1) * rows, lanes])
        own = jnp.concatenate([own_ref[n * pair + i] for i in range(pair)], axis=1)
        totals[0] += jnp.dot(own, strip, preferred_element_type=F32)
        copies[n].wait()
        other = jnp.concatenate([chunks[n, i] for i in range(pair)], axis=1)
        totals[1] += jnp.dot(other, strip, preferred_element_type=F32)
    joined[pl.ds(pl.multiple_of(layer * half, half), half), :] = totals[0]
    joined[pl.ds(pl.multiple_of((1 - layer) * half, half), half), :] = totals[1]
    col = col_ref[0]
    square = decode(strip_ref[pl.ds(pl.multiple_of(col * side, side), side), lanes])
    turned[...] = ((3.0 * square.astype(F32) - 2.0 * joined[...]) * (bound * STEP)).T
    result = turned[pl.ds(pl.multiple_of(layer * (width - half), 8), half), :]
    tiles = half // TILE
    mask = masked_rows(pattern_ref, layer * tiles, tiles, side, False)
    out_ref[...] = (result * mask).astype(BF16)


def shards(density, product_pattern):
    layers = lax.axis_size("layer")
    layer = jnp.reshape(lax.axis_index("layer"), (1,))
    col = jnp.reshape(lax.axis_index("col"), (1,))
    rows, cols = lax.axis_size("row"), lax.axis_size("col")
    side = density.shape[0]
    half = side // layers
    width = -(-half // 128) * 128
    pair = 2
    bound = 2.0
    square_bound = 2.0 ** (2 + (side * rows - 1).bit_length() - 1)
    vmem = pl.BlockSpec(memory_space=pltpu.VMEM)
    smem = pl.BlockSpec(memory_space=pltpu.SMEM)
    hbm = pl.BlockSpec(memory_space=pltpu.HBM)
    claims = [pltpu.CompilerParams(vmem_limit_bytes=n << 20) for n in (56, 56, 24)]
    copies, code = pl.pallas_call(
        functools.partial(start_kernel, bound=bound),
        out_shape=(
            jax.ShapeDtypeStruct((rows, half, side), BF16),
            jax.ShapeDtypeStruct((half, side), jnp.int16),
        ),
        in_specs=[smem, vmem],
        out_specs=(hbm, vmem),
        scratch_shapes=[
            pltpu.VMEM((side, side), F32),
            pltpu.VMEM((half, side), BF16),
            pltpu.SemaphoreType.DMA((rows,)),
        ],
        compiler_params=claims[0],
    )(layer, density)
    right = lax.all_to_all(copies, "row", 0, 0)
    left = lax.all_gather(code, ("col", "layer"), tiled=True)
    right, left = lax.optimization_barrier((right, left))
    code = pl.pallas_call(
        functools.partial(square_kernel, pair=pair, bounds=(bound, square_bound)),
        out_shape=jax.ShapeDtypeStruct((half, side), jnp.int16),
        in_specs=[smem, smem, hbm, hbm],
        out_specs=vmem,
        scratch_shapes=[
            pltpu.VMEM((rows // pair, pair, half, side), BF16),
            pltpu.VMEM((cols // pair, pair * side, side), jnp.int16),
            pltpu.SemaphoreType.DMA((rows // pair,)),
            pltpu.SemaphoreType.DMA((cols // pair,)),
        ],
        compiler_params=claims[1],
    )(layer, product_pattern, right, left)
    other = lax.ppermute(right, "layer", [(i, layers - 1 - i) for i in range(layers)])
    strip = lax.all_gather(code, ("col", "layer"), tiled=True)
    return pl.pallas_call(
        functools.partial(cube_kernel, pair=pair, bound=square_bound),
        out_shape=jax.ShapeDtypeStruct((half, side), BF16),
        in_specs=[smem, smem, smem, vmem, hbm, vmem],
        out_specs=vmem,
        scratch_shapes=[
            pltpu.VMEM((side, width), F32),
            pltpu.VMEM((width, side), F32),
            pltpu.VMEM((rows // pair, pair, half, side), BF16),
            pltpu.SemaphoreType.DMA((rows // pair,)),
        ],
        compiler_params=claims[2],
    )(layer, col, product_pattern, right, other, strip)


def solution(mesh):
    placed = (P("row", "col"), P("row", "col"))
    return jax.shard_map(
        shards, mesh=mesh, in_specs=placed, out_specs=P(("row", "layer"), "col"), check_vma=False
    )
```

```python
import functools

import jax
import jax.numpy as jnp
from jax import lax
from jax.experimental import pallas as pl
from jax.experimental.pallas import tpu as pltpu
from jax.sharding import PartitionSpec as P

TILE = 64
STEP = 2.0**-15
F32, BF16 = jnp.float32, jnp.bfloat16


def encode(values, bound, power):
    size = jnp.abs(values) * (1.0 / bound)
    level = jnp.exp(jnp.log(jnp.maximum(size, 1e-37)) * (1.0 / power)) * (1.0 / STEP) + 0.5
    level = jnp.where(size > 1e-36, jnp.minimum(level, 32767.0), 0.0)
    return jnp.where(values < 0, -level, level).astype(jnp.int32).astype(jnp.int16)


def decode7(codes):
    q = codes.astype(jnp.int32).astype(F32)
    q2 = q * q
    q4 = q2 * q2
    return ((q4 * q2) * q).astype(BF16)


def decode17(codes):
    q = codes.astype(jnp.int32).astype(F32)
    s2 = (q * q) * (STEP * STEP)
    s4 = s2 * s2
    s8 = s4 * s4
    return ((s8 * s8) * q).astype(BF16)


def chunk_copies(source, chunks, sems):
    rows = chunks.shape[1]
    return [
        pltpu.make_async_copy(source.at[pl.ds(n * rows, rows)], chunks.at[n], sems.at[n])
        for n in range(chunks.shape[0])
    ]


def masked_rows(pattern_ref, first, count, columns, transposed):
    lane_tile = lax.broadcasted_iota(jnp.int32, (TILE, columns), 1) // TILE
    out = []
    for i in range(count):
        row = jnp.zeros((TILE, columns), F32)
        for j in range(columns // TILE):
            here = pattern_ref[j, first + i] if transposed else pattern_ref[first + i, j]
            row = jnp.where(lane_tile == j, here.astype(F32), row)
        out.append(row)
    return jnp.concatenate(out, axis=0)


def start_kernel(layer_ref, block_ref, copies_ref, code_ref, turned, mine, sems, *, bound):
    half = code_ref.shape[0]
    turned[...] = block_ref[...].astype(F32).T
    values = turned[pl.ds(pl.multiple_of(layer_ref[0] * half, half), half), :]
    mine[...] = values.astype(BF16)
    copies = [
        pltpu.make_async_copy(mine, copies_ref.at[n], sems.at[n])
        for n in range(copies_ref.shape[0])
    ]
    for copy in copies:
        copy.start()
    code_ref[...] = encode(values, bound, 7)
    for copy in copies:
        copy.wait()


def square_kernel(
    layer_ref,
    pattern_ref,
    right_ref,
    left_ref,
    code_ref,
    right_chunks,
    left_chunks,
    right_sems,
    left_sems,
    *,
    pair,
    group,
    bounds,
):
    half, side = code_ref.shape
    rights = chunk_copies(right_ref, right_chunks, right_sems)
    lefts = chunk_copies(left_ref, left_chunks, left_sems)
    for left_copy, right_copy in zip(lefts, rights):
        left_copy.start()
        right_copy.start()
    tiles = half // TILE
    mask = masked_rows(pattern_ref, layer_ref[0] * tiles, tiles, side, True)
    total = jnp.zeros((half, side), F32)
    for first in range(0, len(lefts), group):
        for n in range(first, first + group):
            lefts[n].wait()
            rights[n].wait()
        for n in range(first, first + group):
            right = jnp.concatenate([right_chunks[n, i] for i in range(pair)], axis=1)
            total += jnp.dot(right, decode7(left_chunks[n]), preferred_element_type=F32)
    squared = (total * (bounds[0] * STEP**7) * mask).astype(BF16).astype(F32)
    code_ref[...] = encode(squared, bounds[1], 17)


def cube_kernel(
    layer_ref,
    col_ref,
    pattern_ref,
    own_ref,
    other_ref,
    strip_ref,
    out_ref,
    joined,
    turned,
    chunks,
    sems,
    *,
    pair,
    bound,
):
    layer = layer_ref[0]
    blocks, half, side = own_ref.shape
    copies = chunk_copies(other_ref, chunks, sems)
    for copy in copies:
        copy.start()
    rows = pair * side
    width = joined.shape[1]
    lanes = pl.ds(pl.multiple_of(layer * (side - width), 128), width)
    totals = [jnp.zeros((half, width), F32), jnp.zeros((half, width), F32)]
    for n in range(blocks // pair):
        strip = decode17(strip_ref[n * rows : (n + 1) * rows, lanes])
        own = jnp.concatenate([own_ref[n * pair + i] for i in range(pair)], axis=1)
        totals[0] += jnp.dot(own, strip, preferred_element_type=F32)
        copies[n].wait()
        other = jnp.concatenate([chunks[n, i] for i in range(pair)], axis=1)
        totals[1] += jnp.dot(other, strip, preferred_element_type=F32)
    joined[pl.ds(pl.multiple_of(layer * half, half), half), :] = totals[0]
    joined[pl.ds(pl.multiple_of((1 - layer) * half, half), half), :] = totals[1]
    col = col_ref[0]
    square = decode17(strip_ref[pl.ds(pl.multiple_of(col * side, side), side), lanes])
    turned[...] = ((3.0 * square.astype(F32) - 2.0 * joined[...]) * (bound * STEP)).T
    result = turned[pl.ds(pl.multiple_of(layer * (width - half), 8), half), :]
    tiles = half // TILE
    mask = masked_rows(pattern_ref, layer * tiles, tiles, side, False)
    out_ref[...] = (result * mask).astype(BF16)


def shards(density, product_pattern):
    layers = lax.axis_size("layer")
    layer = jnp.reshape(lax.axis_index("layer"), (1,))
    col = jnp.reshape(lax.axis_index("col"), (1,))
    rows, cols = lax.axis_size("row"), lax.axis_size("col")
    side = density.shape[0]
    half = side // layers
    width = -(-half // 128) * 128
    pair = 2
    bound = 2.0
    square_bound = 2.0 ** (2 + (side * rows - 1).bit_length() - 1)
    vmem = pl.BlockSpec(memory_space=pltpu.VMEM)
    smem = pl.BlockSpec(memory_space=pltpu.SMEM)
    hbm = pl.BlockSpec(memory_space=pltpu.HBM)
    claims = [pltpu.CompilerParams(vmem_limit_bytes=n << 20) for n in (56, 56, 24)]
    copies, code = pl.pallas_call(
        functools.partial(start_kernel, bound=bound),
        out_shape=(
            jax.ShapeDtypeStruct((rows, half, side), BF16),
            jax.ShapeDtypeStruct((half, side), jnp.int16),
        ),
        in_specs=[smem, vmem],
        out_specs=(hbm, vmem),
        scratch_shapes=[
            pltpu.VMEM((side, side), F32),
            pltpu.VMEM((half, side), BF16),
            pltpu.SemaphoreType.DMA((rows,)),
        ],
        compiler_params=claims[0],
    )(layer, density)
    right = lax.all_to_all(copies, "row", 0, 0)
    left = lax.all_gather(code, ("col", "layer"), tiled=True)
    right, left = lax.optimization_barrier((right, left))
    code = pl.pallas_call(
        functools.partial(square_kernel, pair=pair, group=2, bounds=(bound, square_bound)),
        out_shape=jax.ShapeDtypeStruct((half, side), jnp.int16),
        in_specs=[smem, smem, hbm, hbm],
        out_specs=vmem,
        scratch_shapes=[
            pltpu.VMEM((rows // pair, pair, half, side), BF16),
            pltpu.VMEM((cols // pair, pair * side, side), jnp.int16),
            pltpu.SemaphoreType.DMA((rows // pair,)),
            pltpu.SemaphoreType.DMA((cols // pair,)),
        ],
        compiler_params=claims[1],
    )(layer, product_pattern, right, left)
    other = lax.ppermute(right, "layer", [(i, layers - 1 - i) for i in range(layers)])
    strip = lax.all_gather(code, ("col", "layer"), tiled=True)
    return pl.pallas_call(
        functools.partial(cube_kernel, pair=pair, bound=square_bound),
        out_shape=jax.ShapeDtypeStruct((half, side), BF16),
        in_specs=[smem, smem, smem, vmem, hbm, vmem],
        out_specs=vmem,
        scratch_shapes=[
            pltpu.VMEM((side, width), F32),
            pltpu.VMEM((width, side), F32),
            pltpu.VMEM((rows // pair, pair, half, side), BF16),
            pltpu.SemaphoreType.DMA((rows // pair,)),
        ],
        compiler_params=claims[2],
    )(layer, col, product_pattern, right, other, strip)


def solution(mesh):
    placed = (P("row", "col"), P("row", "col"))
    return jax.shard_map(
        shards, mesh=mesh, in_specs=placed, out_specs=P(("row", "layer"), "col"), check_vma=False
    )
```

```python
import functools

import jax
import jax.numpy as jnp
from jax import lax
from jax.experimental import pallas as pl
from jax.experimental.pallas import tpu as pltpu
from jax.sharding import PartitionSpec as P

TILE = 64
STEP = 2.0**-15
F32, BF16 = jnp.float32, jnp.bfloat16


def encode(values, bound, power):
    size = jnp.abs(values) * (1.0 / bound)
    level = jnp.exp(jnp.log(jnp.maximum(size, 1e-37)) * (1.0 / power)) * (1.0 / STEP) + 0.5
    level = jnp.where(size > 1e-36, jnp.minimum(level, 32767.0), 0.0)
    return jnp.where(values < 0, -level, level).astype(jnp.int32).astype(jnp.int16)


def decode7(codes):
    q = codes.astype(jnp.int32).astype(F32)
    q2 = q * q
    q4 = q2 * q2
    return ((q4 * q2) * q).astype(BF16)


def decode17(codes):
    q = codes.astype(jnp.int32).astype(F32)
    s2 = (q * q) * (STEP * STEP)
    s4 = s2 * s2
    s8 = s4 * s4
    return ((s8 * s8) * q).astype(BF16)


def chunk_copies(source, chunks, sems):
    rows = chunks.shape[1]
    return [
        pltpu.make_async_copy(source.at[pl.ds(n * rows, rows)], chunks.at[n], sems.at[n])
        for n in range(chunks.shape[0])
    ]


def masked_rows(pattern_ref, first, count, columns, transposed):
    lane_tile = lax.broadcasted_iota(jnp.int32, (TILE, columns), 1) // TILE
    out = []
    for i in range(count):
        row = jnp.zeros((TILE, columns), F32)
        for j in range(columns // TILE):
            here = pattern_ref[j, first + i] if transposed else pattern_ref[first + i, j]
            row = jnp.where(lane_tile == j, here.astype(F32), row)
        out.append(row)
    return jnp.concatenate(out, axis=0)


def start_kernel(layer_ref, block_ref, copies_ref, code_ref, turned, mine, sems, *, bound):
    half = code_ref.shape[0]
    turned[...] = block_ref[...].astype(F32).T
    values = turned[pl.ds(pl.multiple_of(layer_ref[0] * half, half), half), :]
    mine[...] = values.astype(BF16)
    copies = [
        pltpu.make_async_copy(mine, copies_ref.at[n], sems.at[n])
        for n in range(copies_ref.shape[0])
    ]
    for copy in copies:
        copy.start()
    code_ref[...] = encode(values, bound, 7)
    for copy in copies:
        copy.wait()


def square_kernel(
    layer_ref, pattern_ref, right_ref, left_ref, code_ref, chunks, sems, *, pair, group, bounds
):
    half, side = code_ref.shape
    copies = chunk_copies(left_ref, chunks, sems)
    for copy in copies:
        copy.start()
    tiles = half // TILE
    mask = masked_rows(pattern_ref, layer_ref[0] * tiles, tiles, side, True)
    total = jnp.zeros((half, side), F32)
    for n in range(len(copies)):
        if n % group == 0:
            for copy in copies[n : n + group]:
                copy.wait()
        right = jnp.concatenate([right_ref[n * pair + i] for i in range(pair)], axis=1)
        total += jnp.dot(right, decode7(chunks[n]), preferred_element_type=F32)
    squared = (total * (bounds[0] * STEP**7) * mask).astype(BF16).astype(F32)
    code_ref[...] = encode(squared, bounds[1], 17)


def cube_kernel(
    layer_ref,
    col_ref,
    pattern_ref,
    own_ref,
    other_ref,
    strip_ref,
    out_ref,
    joined,
    turned,
    chunks,
    sems,
    *,
    pair,
    group,
    bound,
):
    layer = layer_ref[0]
    blocks, half, side = own_ref.shape
    copies = chunk_copies(other_ref, chunks, sems)
    for copy in copies:
        copy.start()
    rows = pair * side
    width = joined.shape[1]
    lanes = pl.ds(pl.multiple_of(layer * (side - width), 128), width)
    total = jnp.zeros((side, width), F32)
    for n in range(blocks // pair):
        if n % group == 0:
            for copy in copies[n : n + group]:
                copy.wait()
        strip = decode17(strip_ref[n * rows : (n + 1) * rows, lanes])
        both = jnp.concatenate(
            [
                jnp.concatenate([own_ref[n * pair + i], chunks[n, i]], axis=0)
                for i in range(pair)
            ],
            axis=1,
        )
        total += jnp.dot(both, strip, preferred_element_type=F32)
    joined[pl.ds(pl.multiple_of(layer * half, half), half), :] = total[:half]
    joined[pl.ds(pl.multiple_of((1 - layer) * half, half), half), :] = total[half:]
    col = col_ref[0]
    square = decode17(strip_ref[pl.ds(pl.multiple_of(col * side, side), side), lanes])
    turned[...] = ((3.0 * square.astype(F32) - 2.0 * joined[...]) * (bound * STEP)).T
    result = turned[pl.ds(pl.multiple_of(layer * (width - half), 8), half), :]
    tiles = half // TILE
    mask = masked_rows(pattern_ref, layer * tiles, tiles, side, False)
    out_ref[...] = (result * mask).astype(BF16)


def shards(density, product_pattern):
    layers = lax.axis_size("layer")
    layer = jnp.reshape(lax.axis_index("layer"), (1,))
    col = jnp.reshape(lax.axis_index("col"), (1,))
    rows, cols = lax.axis_size("row"), lax.axis_size("col")
    side = density.shape[0]
    half = side // layers
    width = -(-half // 128) * 128
    pair = 2
    bound = 2.0
    square_bound = 2.0 ** (2 + (side * rows - 1).bit_length() - 1)
    vmem = pl.BlockSpec(memory_space=pltpu.VMEM)
    smem = pl.BlockSpec(memory_space=pltpu.SMEM)
    hbm = pl.BlockSpec(memory_space=pltpu.HBM)
    claims = [pltpu.CompilerParams(vmem_limit_bytes=n << 20) for n in (56, 50, 24)]
    copies, code = pl.pallas_call(
        functools.partial(start_kernel, bound=bound),
        out_shape=(
            jax.ShapeDtypeStruct((rows, half, side), BF16),
            jax.ShapeDtypeStruct((half, side), jnp.int16),
        ),
        in_specs=[smem, vmem],
        out_specs=(hbm, vmem),
        scratch_shapes=[
            pltpu.VMEM((side, side), F32),
            pltpu.VMEM((half, side), BF16),
            pltpu.SemaphoreType.DMA((rows,)),
        ],
        compiler_params=claims[0],
    )(layer, density)
    right = lax.all_to_all(copies, "row", 0, 0)
    left = lax.all_gather(code, ("col", "layer"), tiled=True)
    right, left = lax.optimization_barrier((right, left))
    code = pl.pallas_call(
        functools.partial(square_kernel, pair=pair, group=2, bounds=(bound, square_bound)),
        out_shape=jax.ShapeDtypeStruct((half, side), jnp.int16),
        in_specs=[smem, smem, vmem, hbm],
        out_specs=vmem,
        scratch_shapes=[
            pltpu.VMEM((cols // pair, pair * side, side), jnp.int16),
            pltpu.SemaphoreType.DMA((cols // pair,)),
        ],
        compiler_params=claims[1],
    )(layer, product_pattern, right, left)
    other = lax.ppermute(right, "layer", [(i, layers - 1 - i) for i in range(layers)])
    strip = lax.all_gather(code, ("col", "layer"), tiled=True)
    return pl.pallas_call(
        functools.partial(cube_kernel, pair=pair, group=8, bound=square_bound),
        out_shape=jax.ShapeDtypeStruct((half, side), BF16),
        in_specs=[smem, smem, smem, vmem, hbm, vmem],
        out_specs=vmem,
        scratch_shapes=[
            pltpu.VMEM((side, width), F32),
            pltpu.VMEM((width, side), F32),
            pltpu.VMEM((rows // pair, pair, half, side), BF16),
            pltpu.SemaphoreType.DMA((rows // pair,)),
        ],
        compiler_params=claims[2],
    )(layer, col, product_pattern, right, other, strip)


def solution(mesh):
    placed = (P("row", "col"), P("row", "col"))
    return jax.shard_map(
        shards, mesh=mesh, in_specs=placed, out_specs=P(("row", "layer"), "col"), check_vma=False
    )
```

```python
import functools

import jax
import jax.numpy as jnp
from jax import lax
from jax.experimental import pallas as pl
from jax.experimental.pallas import tpu as pltpu
from jax.sharding import PartitionSpec as P

TILE = 64
STEP = 2.0**-15
F32, BF16 = jnp.float32, jnp.bfloat16


def encode(values, bound, power):
    size = jnp.abs(values) * (1.0 / bound)
    level = jnp.exp(jnp.log(jnp.maximum(size, 1e-37)) * (1.0 / power)) * (1.0 / STEP) + 0.5
    level = jnp.where(size > 1e-36, jnp.minimum(level, 32767.0), 0.0)
    return jnp.where(values < 0, -level, level).astype(jnp.int32).astype(jnp.int16)


def decode7(codes):
    q = codes.astype(jnp.int32).astype(F32)
    q2 = q * q
    q4 = q2 * q2
    return ((q4 * q2) * q).astype(BF16)


def decode17(codes):
    q = codes.astype(jnp.int32).astype(F32)
    s2 = (q * q) * (STEP * STEP)
    s4 = s2 * s2
    s8 = s4 * s4
    return ((s8 * s8) * q).astype(BF16)


def chunk_copies(source, chunks, sems):
    rows = chunks.shape[1]
    return [
        pltpu.make_async_copy(source.at[pl.ds(n * rows, rows)], chunks.at[n], sems.at[n])
        for n in range(chunks.shape[0])
    ]


def masked_rows(pattern_ref, first, count, columns, transposed):
    lane_tile = lax.broadcasted_iota(jnp.int32, (TILE, columns), 1) // TILE
    out = []
    for i in range(count):
        row = jnp.zeros((TILE, columns), F32)
        for j in range(columns // TILE):
            here = pattern_ref[j, first + i] if transposed else pattern_ref[first + i, j]
            row = jnp.where(lane_tile == j, here.astype(F32), row)
        out.append(row)
    return jnp.concatenate(out, axis=0)


def start_kernel(layer_ref, block_ref, copies_ref, code_ref, turned, mine, sems, *, bound):
    half = code_ref.shape[0]
    turned[...] = block_ref[...].astype(F32).T
    values = turned[pl.ds(pl.multiple_of(layer_ref[0] * half, half), half), :]
    mine[...] = values.astype(BF16)
    copies = [
        pltpu.make_async_copy(mine, copies_ref.at[n], sems.at[n])
        for n in range(copies_ref.shape[0])
    ]
    for copy in copies:
        copy.start()
    code_ref[...] = encode(values, bound, 7)
    for copy in copies:
        copy.wait()


def square_kernel(
    layer_ref, pattern_ref, right_ref, left_ref, code_ref, chunks, sems, *, pair, group, bounds
):
    half, side = code_ref.shape
    copies = chunk_copies(left_ref, chunks, sems)
    for copy in copies:
        copy.start()
    tiles = half // TILE
    mask = masked_rows(pattern_ref, layer_ref[0] * tiles, tiles, side, True)
    total = jnp.zeros((half, side), F32)
    for n in range(len(copies)):
        if n % group == 0:
            for copy in copies[n : n + group]:
                copy.wait()
        right = jnp.concatenate([right_ref[n * pair + i] for i in range(pair)], axis=1)
        total += jnp.dot(right, decode7(chunks[n]), preferred_element_type=F32)
    squared = (total * (bounds[0] * STEP**7) * mask).astype(BF16).astype(F32)
    code_ref[...] = encode(squared, bounds[1], 17)


def cube_kernel(
    layer_ref,
    col_ref,
    pattern_ref,
    own_ref,
    other_ref,
    strip_ref,
    out_ref,
    joined,
    turned,
    chunks,
    sems,
    *,
    pair,
    lead,
    bound,
):
    layer = layer_ref[0]
    blocks, half, side = own_ref.shape
    copies = chunk_copies(other_ref, chunks, sems)
    for copy in copies:
        copy.start()
    rows = pair * side
    width = joined.shape[1]
    lanes = pl.ds(pl.multiple_of(layer * (side - width), 128), width)
    strips = []
    total = jnp.zeros((half, width), F32)
    for n in range(lead):
        strips.append(decode17(strip_ref[n * rows : (n + 1) * rows, lanes]))
        own = jnp.concatenate([own_ref[n * pair + i] for i in range(pair)], axis=1)
        total += jnp.dot(own, strips[n], preferred_element_type=F32)
    for copy in copies:
        copy.wait()
    others = jnp.zeros((half, width), F32)
    for n in range(lead):
        other = jnp.concatenate([chunks[n, i] for i in range(pair)], axis=1)
        others += jnp.dot(other, strips[n], preferred_element_type=F32)
    total = jnp.concatenate([total, others], axis=0)
    for n in range(lead, blocks // pair):
        strip = decode17(strip_ref[n * rows : (n + 1) * rows, lanes])
        both = jnp.concatenate(
            [
                jnp.concatenate([own_ref[n * pair + i], chunks[n, i]], axis=0)
                for i in range(pair)
            ],
            axis=1,
        )
        total += jnp.dot(both, strip, preferred_element_type=F32)
    joined[pl.ds(pl.multiple_of(layer * half, half), half), :] = total[:half]
    joined[pl.ds(pl.multiple_of((1 - layer) * half, half), half), :] = total[half:]
    col = col_ref[0]
    square = decode17(strip_ref[pl.ds(pl.multiple_of(col * side, side), side), lanes])
    turned[...] = ((3.0 * square.astype(F32) - 2.0 * joined[...]) * (bound * STEP)).T
    result = turned[pl.ds(pl.multiple_of(layer * (width - half), 8), half), :]
    tiles = half // TILE
    mask = masked_rows(pattern_ref, layer * tiles, tiles, side, False)
    out_ref[...] = (result * mask).astype(BF16)


def shards(density, product_pattern):
    layers = lax.axis_size("layer")
    layer = jnp.reshape(lax.axis_index("layer"), (1,))
    col = jnp.reshape(lax.axis_index("col"), (1,))
    rows, cols = lax.axis_size("row"), lax.axis_size("col")
    side = density.shape[0]
    half = side // layers
    width = -(-half // 128) * 128
    pair = 2
    bound = 2.0
    square_bound = 2.0 ** (2 + (side * rows - 1).bit_length() - 1)
    vmem = pl.BlockSpec(memory_space=pltpu.VMEM)
    smem = pl.BlockSpec(memory_space=pltpu.SMEM)
    hbm = pl.BlockSpec(memory_space=pltpu.HBM)
    claims = [pltpu.CompilerParams(vmem_limit_bytes=n << 20) for n in (24, 50, 24)]
    copies, code = pl.pallas_call(
        functools.partial(start_kernel, bound=bound),
        out_shape=(
            pltpu.HBM((rows, half, side), BF16),
            jax.ShapeDtypeStruct((half, side), jnp.int16),
        ),
        in_specs=[smem, vmem],
        out_specs=(hbm, vmem),
        scratch_shapes=[
            pltpu.VMEM((side, side), F32),
            pltpu.VMEM((half, side), BF16),
            pltpu.SemaphoreType.DMA((rows,)),
        ],
        compiler_params=claims[0],
    )(layer, density)
    right = lax.all_to_all(copies, "row", 0, 0)
    left = lax.all_gather(code, ("col", "layer"), tiled=True)
    right, left = lax.optimization_barrier((right, left))
    code = pl.pallas_call(
        functools.partial(square_kernel, pair=pair, group=2, bounds=(bound, square_bound)),
        out_shape=jax.ShapeDtypeStruct((half, side), jnp.int16),
        in_specs=[smem, smem, vmem, hbm],
        out_specs=vmem,
        scratch_shapes=[
            pltpu.VMEM((cols // pair, pair * side, side), jnp.int16),
            pltpu.SemaphoreType.DMA((cols // pair,)),
        ],
        compiler_params=claims[1],
    )(layer, product_pattern, right, left)
    other = lax.ppermute(right, "layer", [(i, layers - 1 - i) for i in range(layers)])
    strip = lax.all_gather(code, ("col", "layer"), tiled=True)
    return pl.pallas_call(
        functools.partial(cube_kernel, pair=pair, lead=2, bound=square_bound),
        out_shape=jax.ShapeDtypeStruct((half, side), BF16),
        in_specs=[smem, smem, smem, vmem, hbm, vmem],
        out_specs=vmem,
        scratch_shapes=[
            pltpu.VMEM((side, width), F32),
            pltpu.VMEM((width, side), F32),
            pltpu.VMEM((rows // pair, pair, half, side), BF16),
            pltpu.SemaphoreType.DMA((rows // pair,)),
        ],
        compiler_params=claims[2],
    )(layer, col, product_pattern, right, other, strip)


def solution(mesh):
    placed = (P("row", "col"), P("row", "col"))
    return jax.shard_map(
        shards, mesh=mesh, in_specs=placed, out_specs=P(("row", "layer"), "col"), check_vma=False
    )
```

```python
import functools

import jax
import jax.numpy as jnp
from jax import lax
from jax.experimental import pallas as pl
from jax.experimental.pallas import tpu as pltpu
from jax.sharding import PartitionSpec as P

TILE = 64
STEP = 2.0**-15
F32, BF16 = jnp.float32, jnp.bfloat16


def encode(values, bound, power):
    size = jnp.abs(values) * (1.0 / bound)
    level = jnp.exp(jnp.log(jnp.maximum(size, 1e-37)) * (1.0 / power)) * (1.0 / STEP) + 0.5
    level = jnp.where(size > 1e-36, jnp.minimum(level, 32767.0), 0.0)
    return jnp.where(values < 0, -level, level).astype(jnp.int32).astype(jnp.int16)


def decode7(codes):
    q = codes.astype(jnp.int32).astype(F32)
    q2 = q * q
    q4 = q2 * q2
    return ((q4 * q2) * q).astype(BF16)


def decode17(codes):
    q = codes.astype(jnp.int32).astype(F32)
    s2 = (q * q) * (STEP * STEP)
    s4 = s2 * s2
    s8 = s4 * s4
    return ((s8 * s8) * q).astype(BF16)


def chunk_copies(source, chunks, sems):
    rows = chunks.shape[1]
    return [
        pltpu.make_async_copy(source.at[pl.ds(n * rows, rows)], chunks.at[n], sems.at[n])
        for n in range(chunks.shape[0])
    ]


def masked_rows(pattern_ref, first, count, columns, transposed):
    lane_tile = lax.broadcasted_iota(jnp.int32, (TILE, columns), 1) // TILE
    out = []
    for i in range(count):
        row = jnp.zeros((TILE, columns), F32)
        for j in range(columns // TILE):
            here = pattern_ref[j, first + i] if transposed else pattern_ref[first + i, j]
            row = jnp.where(lane_tile == j, here.astype(F32), row)
        out.append(row)
    return jnp.concatenate(out, axis=0)


def start_kernel(
    layer_ref, block_ref, copies_ref, code_ref, fetched, turned, mine, sems, fetch_sem, *, bound
):
    half, side = code_ref.shape
    width = fetched.shape[1]
    lanes = pl.ds(pl.multiple_of(layer_ref[0] * (side - width), 128), width)
    fetch = pltpu.make_async_copy(block_ref.at[:, lanes], fetched, fetch_sem)
    fetch.start()
    fetch.wait()
    turned[...] = fetched[...].astype(F32).T
    values = turned[pl.ds(pl.multiple_of(layer_ref[0] * (width - half), 8), half), :]
    mine[...] = values.astype(BF16)
    copies = [
        pltpu.make_async_copy(mine, copies_ref.at[n], sems.at[n])
        for n in range(copies_ref.shape[0])
    ]
    for copy in copies:
        copy.start()
    code_ref[...] = encode(values, bound, 7)
    for copy in copies:
        copy.wait()


def square_kernel(
    layer_ref, pattern_ref, right_ref, left_ref, code_ref, chunks, sems, *, pair, group, bounds
):
    half, side = code_ref.shape
    copies = chunk_copies(left_ref, chunks, sems)
    for copy in copies:
        copy.start()
    tiles = half // TILE
    mask = masked_rows(pattern_ref, layer_ref[0] * tiles, tiles, side, True)
    total = jnp.zeros((half, side), F32)
    for n in range(len(copies)):
        if n % group == 0:
            for copy in copies[n : n + group]:
                copy.wait()
        right = jnp.concatenate([right_ref[n * pair + i] for i in range(pair)], axis=1)
        total += jnp.dot(right, decode7(chunks[n]), preferred_element_type=F32)
    squared = (total * (bounds[0] * STEP**7) * mask).astype(BF16).astype(F32)
    code_ref[...] = encode(squared, bounds[1], 17)


def cube_kernel(
    layer_ref,
    col_ref,
    pattern_ref,
    own_ref,
    other_ref,
    strip_ref,
    out_ref,
    joined,
    turned,
    chunks,
    sems,
    *,
    pair,
    lead,
    bound,
):
    layer = layer_ref[0]
    blocks, half, side = own_ref.shape
    copies = chunk_copies(other_ref, chunks, sems)
    for copy in copies:
        copy.start()
    rows = pair * side
    width = joined.shape[1]
    lanes = pl.ds(pl.multiple_of(layer * (side - width), 128), width)
    strips = []
    total = jnp.zeros((half, width), F32)
    for n in range(lead):
        strips.append(decode17(strip_ref[n * rows : (n + 1) * rows, lanes]))
        own = jnp.concatenate([own_ref[n * pair + i] for i in range(pair)], axis=1)
        total += jnp.dot(own, strips[n], preferred_element_type=F32)
    for copy in copies:
        copy.wait()
    others = jnp.zeros((half, width), F32)
    for n in range(lead):
        other = jnp.concatenate([chunks[n, i] for i in range(pair)], axis=1)
        others += jnp.dot(other, strips[n], preferred_element_type=F32)
    total = jnp.concatenate([total, others], axis=0)
    for n in range(lead, blocks // pair):
        strip = decode17(strip_ref[n * rows : (n + 1) * rows, lanes])
        both = jnp.concatenate(
            [
                jnp.concatenate([own_ref[n * pair + i], chunks[n, i]], axis=0)
                for i in range(pair)
            ],
            axis=1,
        )
        total += jnp.dot(both, strip, preferred_element_type=F32)
    joined[pl.ds(pl.multiple_of(layer * half, half), half), :] = total[:half]
    joined[pl.ds(pl.multiple_of((1 - layer) * half, half), half), :] = total[half:]
    col = col_ref[0]
    square = decode17(strip_ref[pl.ds(pl.multiple_of(col * side, side), side), lanes])
    turned[...] = ((3.0 * square.astype(F32) - 2.0 * joined[...]) * (bound * STEP)).T
    result = turned[pl.ds(pl.multiple_of(layer * (width - half), 8), half), :]
    tiles = half // TILE
    mask = masked_rows(pattern_ref, layer * tiles, tiles, side, False)
    out_ref[...] = (result * mask).astype(BF16)


def shards(density, product_pattern):
    layers = lax.axis_size("layer")
    layer = jnp.reshape(lax.axis_index("layer"), (1,))
    col = jnp.reshape(lax.axis_index("col"), (1,))
    rows, cols = lax.axis_size("row"), lax.axis_size("col")
    side = density.shape[0]
    half = side // layers
    width = -(-half // 128) * 128
    pair = 2
    bound = 2.0
    square_bound = 2.0 ** (2 + (side * rows - 1).bit_length() - 1)
    vmem = pl.BlockSpec(memory_space=pltpu.VMEM)
    smem = pl.BlockSpec(memory_space=pltpu.SMEM)
    hbm = pl.BlockSpec(memory_space=pltpu.HBM)
    claims = [pltpu.CompilerParams(vmem_limit_bytes=n << 20) for n in (56, 50, 24)]
    copies, code = pl.pallas_call(
        functools.partial(start_kernel, bound=bound),
        out_shape=(
            pltpu.HBM((rows, half, side), BF16),
            pltpu.VMEM((half, side), jnp.int16),
        ),
        in_specs=[smem, hbm],
        out_specs=(hbm, vmem),
        scratch_shapes=[
            pltpu.VMEM((side, width), BF16),
            pltpu.VMEM((width, side), F32),
            pltpu.VMEM((half, side), BF16),
            pltpu.SemaphoreType.DMA((rows,)),
            pltpu.SemaphoreType.DMA,
        ],
        compiler_params=claims[0],
    )(layer, density)
    right = lax.all_to_all(copies, "row", 0, 0)
    left = lax.all_gather(code, ("col", "layer"), tiled=True)
    right, left = lax.optimization_barrier((right, left))
    code = pl.pallas_call(
        functools.partial(square_kernel, pair=pair, group=2, bounds=(bound, square_bound)),
        out_shape=jax.ShapeDtypeStruct((half, side), jnp.int16),
        in_specs=[smem, smem, vmem, hbm],
        out_specs=vmem,
        scratch_shapes=[
            pltpu.VMEM((cols // pair, pair * side, side), jnp.int16),
            pltpu.SemaphoreType.DMA((cols // pair,)),
        ],
        compiler_params=claims[1],
    )(layer, product_pattern, right, left)
    other = lax.ppermute(right, "layer", [(i, layers - 1 - i) for i in range(layers)])
    strip = lax.all_gather(code, ("col", "layer"), tiled=True)
    return pl.pallas_call(
        functools.partial(cube_kernel, pair=pair, lead=3, bound=square_bound),
        out_shape=jax.ShapeDtypeStruct((half, side), BF16),
        in_specs=[smem, smem, smem, vmem, hbm, vmem],
        out_specs=vmem,
        scratch_shapes=[
            pltpu.VMEM((side, width), F32),
            pltpu.VMEM((width, side), F32),
            pltpu.VMEM((rows // pair, pair, half, side), BF16),
            pltpu.SemaphoreType.DMA((rows // pair,)),
        ],
        compiler_params=claims[2],
    )(layer, col, product_pattern, right, other, strip)


def solution(mesh):
    placed = (P("row", "col"), P("row", "col"))
    return jax.shard_map(
        shards, mesh=mesh, in_specs=placed, out_specs=P(("row", "layer"), "col"), check_vma=False
    )
```

```python
import functools

import jax
import jax.numpy as jnp
from jax import lax
from jax.experimental import pallas as pl
from jax.experimental.pallas import tpu as pltpu
from jax.sharding import PartitionSpec as P

TILE = 64
STEP = 2.0**-15
F32, BF16 = jnp.float32, jnp.bfloat16


def encode(values, bound, power):
    size = jnp.abs(values) * (1.0 / bound)
    level = jnp.exp(jnp.log(jnp.maximum(size, 1e-37)) * (1.0 / power)) * (1.0 / STEP) + 0.5
    level = jnp.where(size > 1e-36, jnp.minimum(level, 32767.0), 0.0)
    return jnp.where(values < 0, -level, level).astype(jnp.int32).astype(jnp.int16)


def decode7(codes):
    q = codes.astype(jnp.int32).astype(F32)
    q2 = q * q
    q4 = q2 * q2
    return ((q4 * q2) * q).astype(BF16)


def decode17(codes):
    q = codes.astype(jnp.int32).astype(F32)
    s2 = (q * q) * (STEP * STEP)
    s4 = s2 * s2
    s8 = s4 * s4
    return ((s8 * s8) * q).astype(BF16)


def chunk_copies(source, chunks, sems):
    rows = chunks.shape[1]
    return [
        pltpu.make_async_copy(source.at[pl.ds(n * rows, rows)], chunks.at[n], sems.at[n])
        for n in range(chunks.shape[0])
    ]


def masked_rows(pattern_ref, first, count, columns, transposed):
    lane_tile = lax.broadcasted_iota(jnp.int32, (TILE, columns), 1) // TILE
    out = []
    for i in range(count):
        row = jnp.zeros((TILE, columns), F32)
        for j in range(columns // TILE):
            here = pattern_ref[j, first + i] if transposed else pattern_ref[first + i, j]
            row = jnp.where(lane_tile == j, here.astype(F32), row)
        out.append(row)
    return jnp.concatenate(out, axis=0)


def start_kernel(
    layer_ref, block_ref, copies_ref, code_ref, fetched, turned, mine, sems, fetch_sem, *, bound
):
    half, side = code_ref.shape
    width = fetched.shape[1]
    lanes = pl.ds(pl.multiple_of(layer_ref[0] * (side - width), 128), width)
    fetch = pltpu.make_async_copy(block_ref.at[:, lanes], fetched, fetch_sem)
    fetch.start()
    fetch.wait()
    turned[...] = fetched[...].astype(F32).T
    values = turned[pl.ds(pl.multiple_of(layer_ref[0] * (width - half), 8), half), :]
    mine[...] = values.astype(BF16)
    copies = [
        pltpu.make_async_copy(mine, copies_ref.at[n], sems.at[n])
        for n in range(copies_ref.shape[0])
    ]
    for copy in copies:
        copy.start()
    code_ref[...] = encode(values, bound, 7)
    for copy in copies:
        copy.wait()


def square_kernel(
    layer_ref, pattern_ref, right_ref, left_ref, code_ref, chunks, sems, *, pair, group, bounds
):
    half, side = code_ref.shape
    copies = chunk_copies(left_ref, chunks, sems)
    for copy in copies:
        copy.start()
    tiles = half // TILE
    mask = masked_rows(pattern_ref, layer_ref[0] * tiles, tiles, side, True)
    total = jnp.zeros((half, side), F32)
    for n in range(len(copies)):
        if n % group == 0:
            for copy in copies[n : n + group]:
                copy.wait()
        right = jnp.concatenate([right_ref[n * pair + i] for i in range(pair)], axis=1)
        total += jnp.dot(right, decode7(chunks[n]), preferred_element_type=F32)
    squared = (total * (bounds[0] * STEP**7) * mask).astype(BF16).astype(F32)
    code_ref[...] = encode(squared, bounds[1], 17)


def cube_kernel(
    layer_ref,
    col_ref,
    pattern_ref,
    own_ref,
    other_ref,
    strip_ref,
    out_ref,
    joined,
    turned,
    chunks,
    sems,
    *,
    pair,
    lead,
    bound,
):
    layer = layer_ref[0]
    blocks, half, side = own_ref.shape
    copies = chunk_copies(other_ref, chunks, sems)
    for copy in copies:
        copy.start()
    rows = pair * side
    width = joined.shape[1]
    lanes = pl.ds(pl.multiple_of(layer * (side - width), 128), width)
    tiles = half // TILE
    mask = masked_rows(pattern_ref, layer * tiles, tiles, side, False)
    col = col_ref[0]
    square = decode17(strip_ref[pl.ds(pl.multiple_of(col * side, side), side), lanes])
    strips = []
    total = jnp.zeros((half, width), F32)
    for n in range(lead):
        strips.append(decode17(strip_ref[n * rows : (n + 1) * rows, lanes]))
        own = jnp.concatenate([own_ref[n * pair + i] for i in range(pair)], axis=1)
        total += jnp.dot(own, strips[n], preferred_element_type=F32)
    for copy in copies:
        copy.wait()
    others = jnp.zeros((half, width), F32)
    for n in range(lead):
        other = jnp.concatenate([chunks[n, i] for i in range(pair)], axis=1)
        others += jnp.dot(other, strips[n], preferred_element_type=F32)
    total = jnp.concatenate([total, others], axis=0)
    for n in range(lead, blocks // pair):
        strip = decode17(strip_ref[n * rows : (n + 1) * rows, lanes])
        both = jnp.concatenate(
            [
                jnp.concatenate([own_ref[n * pair + i], chunks[n, i]], axis=0)
                for i in range(pair)
            ],
            axis=1,
        )
        total += jnp.dot(both, strip, preferred_element_type=F32)
    joined[pl.ds(pl.multiple_of(layer * half, half), half), :] = total[:half]
    joined[pl.ds(pl.multiple_of((1 - layer) * half, half), half), :] = total[half:]
    turned[...] = ((3.0 * square.astype(F32) - 2.0 * joined[...]) * (bound * STEP)).T
    result = turned[pl.ds(pl.multiple_of(layer * (width - half), 8), half), :]
    out_ref[...] = (result * mask).astype(BF16)


def shards(density, product_pattern):
    layers = lax.axis_size("layer")
    layer = jnp.reshape(lax.axis_index("layer"), (1,))
    col = jnp.reshape(lax.axis_index("col"), (1,))
    rows, cols = lax.axis_size("row"), lax.axis_size("col")
    side = density.shape[0]
    half = side // layers
    width = -(-half // 128) * 128
    pair = 2
    bound = 2.0
    square_bound = 2.0 ** (2 + (side * rows - 1).bit_length() - 1)
    vmem = pl.BlockSpec(memory_space=pltpu.VMEM)
    smem = pl.BlockSpec(memory_space=pltpu.SMEM)
    hbm = pl.BlockSpec(memory_space=pltpu.HBM)
    claims = [pltpu.CompilerParams(vmem_limit_bytes=n << 20) for n in (56, 50, 24)]
    copies, code = pl.pallas_call(
        functools.partial(start_kernel, bound=bound),
        out_shape=(
            pltpu.HBM((rows, half, side), BF16),
            pltpu.VMEM((half, side), jnp.int16),
        ),
        in_specs=[smem, hbm],
        out_specs=(hbm, vmem),
        scratch_shapes=[
            pltpu.VMEM((side, width), BF16),
            pltpu.VMEM((width, side), F32),
            pltpu.VMEM((half, side), BF16),
            pltpu.SemaphoreType.DMA((rows,)),
            pltpu.SemaphoreType.DMA,
        ],
        compiler_params=claims[0],
    )(layer, density)
    right = lax.all_to_all(copies, "row", 0, 0)
    left = lax.all_gather(code, ("col", "layer"), tiled=True)
    right, left = lax.optimization_barrier((right, left))
    code = pl.pallas_call(
        functools.partial(square_kernel, pair=pair, group=2, bounds=(bound, square_bound)),
        out_shape=jax.ShapeDtypeStruct((half, side), jnp.int16),
        in_specs=[smem, smem, vmem, hbm],
        out_specs=vmem,
        scratch_shapes=[
            pltpu.VMEM((cols // pair, pair * side, side), jnp.int16),
            pltpu.SemaphoreType.DMA((cols // pair,)),
        ],
        compiler_params=claims[1],
    )(layer, product_pattern, right, left)
    other = lax.ppermute(right, "layer", [(i, layers - 1 - i) for i in range(layers)])
    strip = lax.all_gather(code, ("col", "layer"), tiled=True)
    return pl.pallas_call(
        functools.partial(cube_kernel, pair=pair, lead=3, bound=square_bound),
        out_shape=jax.ShapeDtypeStruct((half, side), BF16),
        in_specs=[smem, smem, smem, vmem, hbm, vmem],
        out_specs=vmem,
        scratch_shapes=[
            pltpu.VMEM((side, width), F32),
            pltpu.VMEM((width, side), F32),
            pltpu.VMEM((rows // pair, pair, half, side), BF16),
            pltpu.SemaphoreType.DMA((rows // pair,)),
        ],
        compiler_params=claims[2],
    )(layer, col, product_pattern, right, other, strip)


def solution(mesh):
    placed = (P("row", "col"), P("row", "col"))
    return jax.shard_map(
        shards, mesh=mesh, in_specs=placed, out_specs=P(("row", "layer"), "col"), check_vma=False
    )
```

```python
import functools

import jax
import jax.numpy as jnp
from jax import lax
from jax.experimental import pallas as pl
from jax.experimental.pallas import tpu as pltpu
from jax.sharding import PartitionSpec as P

TILE = 64
STEP = 2.0**-15
F32, BF16 = jnp.float32, jnp.bfloat16


def encode(values, bound, power):
    size = jnp.abs(values) * (1.0 / bound)
    level = jnp.exp(jnp.log(jnp.maximum(size, 1e-37)) * (1.0 / power)) * (1.0 / STEP) + 0.5
    level = jnp.where(size > 1e-36, jnp.minimum(level, 32767.0), 0.0)
    return jnp.where(values < 0, -level, level).astype(jnp.int32).astype(jnp.int16)


def decode7(codes):
    q = codes.astype(jnp.int32).astype(F32)
    q2 = q * q
    q4 = q2 * q2
    return ((q4 * q2) * q).astype(BF16)


def decode17(codes):
    q = codes.astype(jnp.int32).astype(F32)
    s2 = (q * q) * (STEP * STEP)
    s4 = s2 * s2
    s8 = s4 * s4
    return ((s8 * s8) * q).astype(BF16)


def chunk_copies(source, chunks, sems):
    rows = chunks.shape[1]
    return [
        pltpu.make_async_copy(source.at[pl.ds(n * rows, rows)], chunks.at[n], sems.at[n])
        for n in range(chunks.shape[0])
    ]


def masked_rows(pattern_ref, first, count, columns, transposed):
    lane_tile = lax.broadcasted_iota(jnp.int32, (TILE, columns), 1) // TILE
    out = []
    for i in range(count):
        row = jnp.zeros((TILE, columns), F32)
        for j in range(columns // TILE):
            here = pattern_ref[j, first + i] if transposed else pattern_ref[first + i, j]
            row = jnp.where(lane_tile == j, here.astype(F32), row)
        out.append(row)
    return jnp.concatenate(out, axis=0)


def start_kernel(
    layer_ref, block_ref, copies_ref, code_ref, fetched, turned, mine, sems, fetch_sem, *, bound
):
    half, side = code_ref.shape
    width = fetched.shape[1]
    lanes = pl.ds(pl.multiple_of(layer_ref[0] * (side - width), 128), width)
    fetch = pltpu.make_async_copy(block_ref.at[:, lanes], fetched, fetch_sem)
    fetch.start()
    fetch.wait()
    turned[...] = fetched[...].astype(F32).T
    values = turned[pl.ds(pl.multiple_of(layer_ref[0] * (width - half), 8), half), :]
    mine[...] = values.astype(BF16)
    copies = [
        pltpu.make_async_copy(mine, copies_ref.at[n], sems.at[n])
        for n in range(copies_ref.shape[0])
    ]
    for copy in copies:
        copy.start()
    code_ref[...] = encode(values, bound, 7)
    for copy in copies:
        copy.wait()


def square_kernel(
    layer_ref, pattern_ref, right_ref, left_ref, code_ref, chunks, sems, *, pair, group, bounds
):
    half, side = code_ref.shape
    copies = chunk_copies(left_ref, chunks, sems)
    for copy in copies:
        copy.start()
    tiles = half // TILE
    mask = masked_rows(pattern_ref, layer_ref[0] * tiles, tiles, side, True)
    total = jnp.zeros((half, side), F32)
    for n in range(len(copies)):
        if n % group == 0:
            for copy in copies[n : n + group]:
                copy.wait()
        right = jnp.concatenate([right_ref[n * pair + i] for i in range(pair)], axis=1)
        total += jnp.dot(right, decode7(chunks[n]), preferred_element_type=F32)
    squared = (total * (bounds[0] * STEP**7) * mask).astype(BF16).astype(F32)
    code_ref[...] = encode(squared, bounds[1], 17)


def cube_kernel(
    layer_ref,
    col_ref,
    pattern_ref,
    own_ref,
    other_ref,
    strip_ref,
    out_ref,
    joined,
    turned,
    chunks,
    sems,
    *,
    pair,
    lead,
    bound,
):
    layer = layer_ref[0]
    blocks, half, side = own_ref.shape
    copies = chunk_copies(other_ref, chunks, sems)
    for copy in copies:
        copy.start()
    rows = pair * side
    width = joined.shape[1]
    lanes = pl.ds(pl.multiple_of(layer * (side - width), 128), width)
    strips = []
    total = jnp.zeros((half, width), F32)
    for n in range(lead):
        strips.append(decode17(strip_ref[n * rows : (n + 1) * rows, lanes]))
        own = jnp.concatenate([own_ref[n * pair + i] for i in range(pair)], axis=1)
        total += jnp.dot(own, strips[n], preferred_element_type=F32)
    for copy in copies:
        copy.wait()
    others = jnp.zeros((half, width), F32)
    for n in range(lead):
        other = jnp.concatenate([chunks[n, i] for i in range(pair)], axis=1)
        others += jnp.dot(other, strips[n], preferred_element_type=F32)
    total = jnp.concatenate([total, others], axis=0)
    for n in range(lead, blocks // pair):
        strip = decode17(strip_ref[n * rows : (n + 1) * rows, lanes])
        both = jnp.concatenate(
            [
                jnp.concatenate([own_ref[n * pair + i], chunks[n, i]], axis=0)
                for i in range(pair)
            ],
            axis=1,
        )
        total += jnp.dot(both, strip, preferred_element_type=F32)
    joined[pl.ds(pl.multiple_of(layer * half, half), half), :] = total[:half]
    joined[pl.ds(pl.multiple_of((1 - layer) * half, half), half), :] = total[half:]
    col = col_ref[0]
    square = decode17(strip_ref[pl.ds(pl.multiple_of(col * side, side), side), lanes])
    turned[...] = ((3.0 * square.astype(F32) - 2.0 * joined[...]) * (bound * STEP)).T
    result = turned[pl.ds(pl.multiple_of(layer * (width - half), 8), half), :]
    tiles = half // TILE
    mask = masked_rows(pattern_ref, layer * tiles, tiles, side, False)
    out_ref[...] = (result * mask).astype(BF16)


def shards(density, product_pattern):
    layers = lax.axis_size("layer")
    layer = jnp.reshape(lax.axis_index("layer"), (1,))
    col = jnp.reshape(lax.axis_index("col"), (1,))
    rows, cols = lax.axis_size("row"), lax.axis_size("col")
    side = density.shape[0]
    half = side // layers
    width = -(-half // 128) * 128
    pair = 2
    bound = 2.0
    square_bound = 2.0 ** (2 + (side * rows - 1).bit_length() - 1)
    vmem = pl.BlockSpec(memory_space=pltpu.VMEM)
    smem = pl.BlockSpec(memory_space=pltpu.SMEM)
    hbm = pl.BlockSpec(memory_space=pltpu.HBM)
    claims = [pltpu.CompilerParams(vmem_limit_bytes=n << 20) for n in (56, 50, 24)]
    copies, code = pl.pallas_call(
        functools.partial(start_kernel, bound=bound),
        out_shape=(
            pltpu.HBM((rows, half, side), BF16),
            pltpu.VMEM((half, side), jnp.int16),
        ),
        in_specs=[smem, hbm],
        out_specs=(hbm, vmem),
        scratch_shapes=[
            pltpu.VMEM((side, width), BF16),
            pltpu.VMEM((width, side), F32),
            pltpu.VMEM((half, side), BF16),
            pltpu.SemaphoreType.DMA((rows,)),
            pltpu.SemaphoreType.DMA,
        ],
        compiler_params=claims[0],
    )(layer, density)
    right = lax.all_to_all(copies, "row", 0, 0)
    left = lax.all_gather(code, ("col", "layer"), tiled=True)
    right, left = lax.optimization_barrier((right, left))
    code = pl.pallas_call(
        functools.partial(square_kernel, pair=pair, group=2, bounds=(bound, square_bound)),
        out_shape=jax.ShapeDtypeStruct((half, side), jnp.int16),
        in_specs=[smem, smem, vmem, hbm],
        out_specs=vmem,
        scratch_shapes=[
            pltpu.VMEM((cols // pair, pair * side, side), jnp.int16),
            pltpu.SemaphoreType.DMA((cols // pair,)),
        ],
        compiler_params=claims[1],
    )(layer, product_pattern, right, left)
    sent, code = lax.optimization_barrier((right, code))
    other = lax.ppermute(sent, "layer", [(i, layers - 1 - i) for i in range(layers)])
    strip = lax.all_gather(code, ("col", "layer"), tiled=True)
    return pl.pallas_call(
        functools.partial(cube_kernel, pair=pair, lead=3, bound=square_bound),
        out_shape=jax.ShapeDtypeStruct((half, side), BF16),
        in_specs=[smem, smem, smem, vmem, hbm, vmem],
        out_specs=vmem,
        scratch_shapes=[
            pltpu.VMEM((side, width), F32),
            pltpu.VMEM((width, side), F32),
            pltpu.VMEM((rows // pair, pair, half, side), BF16),
            pltpu.SemaphoreType.DMA((rows // pair,)),
        ],
        compiler_params=claims[2],
    )(layer, col, product_pattern, right, other, strip)


def solution(mesh):
    placed = (P("row", "col"), P("row", "col"))
    return jax.shard_map(
        shards, mesh=mesh, in_specs=placed, out_specs=P(("row", "layer"), "col"), check_vma=False
    )
```

```python
import functools

import jax
import jax.numpy as jnp
from jax import lax
from jax.experimental import pallas as pl
from jax.experimental.pallas import tpu as pltpu
from jax.sharding import PartitionSpec as P

TILE = 64
STEP = 2.0**-15
F32, BF16 = jnp.float32, jnp.bfloat16


def encode(values, bound, power):
    size = jnp.abs(values) * (1.0 / bound)
    level = jnp.exp(jnp.log(jnp.maximum(size, 1e-37)) * (1.0 / power)) * (1.0 / STEP) + 0.5
    level = jnp.where(size > 1e-36, jnp.minimum(level, 32767.0), 0.0)
    return jnp.where(values < 0, -level, level).astype(jnp.int32).astype(jnp.int16)


def decode7(codes):
    q = codes.astype(jnp.int32).astype(F32)
    q2 = q * q
    q4 = q2 * q2
    return ((q4 * q2) * q).astype(BF16)


def decode17(codes):
    q = codes.astype(jnp.int32).astype(F32)
    s2 = (q * q) * (STEP * STEP)
    s4 = s2 * s2
    s8 = s4 * s4
    return ((s8 * s8) * q).astype(BF16)


def chunk_copies(source, chunks, sems):
    rows = chunks.shape[1]
    return [
        pltpu.make_async_copy(source.at[pl.ds(n * rows, rows)], chunks.at[n], sems.at[n])
        for n in range(chunks.shape[0])
    ]


def masked_rows(pattern_ref, first, count, columns, transposed):
    lane_tile = lax.broadcasted_iota(jnp.int32, (TILE, columns), 1) // TILE
    out = []
    for i in range(count):
        row = jnp.zeros((TILE, columns), F32)
        for j in range(columns // TILE):
            here = pattern_ref[j, first + i] if transposed else pattern_ref[first + i, j]
            row = jnp.where(lane_tile == j, here.astype(F32), row)
        out.append(row)
    return jnp.concatenate(out, axis=0)


def start_kernel(
    layer_ref, block_ref, copies_ref, code_ref, fetched, turned, mine, sems, fetch_sem, *, bound
):
    half, side = code_ref.shape
    width = fetched.shape[1]
    lanes = pl.ds(pl.multiple_of(layer_ref[0] * (side - width), 128), width)
    fetch = pltpu.make_async_copy(block_ref.at[:, lanes], fetched, fetch_sem)
    fetch.start()
    fetch.wait()
    turned[...] = fetched[...].astype(F32).T
    values = turned[pl.ds(pl.multiple_of(layer_ref[0] * (width - half), 8), half), :]
    mine[...] = values.astype(BF16)
    copies = [
        pltpu.make_async_copy(mine, copies_ref.at[n], sems.at[n])
        for n in range(copies_ref.shape[0])
    ]
    for copy in copies:
        copy.start()
    code_ref[...] = encode(values, bound, 7)
    for copy in copies:
        copy.wait()


def square_kernel(
    layer_ref, pattern_ref, right_ref, left_ref, code_ref, chunks, sems, *, pair, group, bounds
):
    half, side = code_ref.shape
    copies = chunk_copies(left_ref, chunks, sems)
    for copy in copies:
        copy.start()
    tiles = half // TILE
    mask = masked_rows(pattern_ref, layer_ref[0] * tiles, tiles, side, True)
    total = jnp.zeros((half, side), F32)
    for n in range(len(copies)):
        if n % group == 0:
            for copy in copies[n : n + group]:
                copy.wait()
        right = jnp.concatenate([right_ref[n * pair + i] for i in range(pair)], axis=1)
        total += jnp.dot(right, decode7(chunks[n]), preferred_element_type=F32)
    squared = (total * (bounds[0] * STEP**7) * mask).astype(BF16).astype(F32)
    code_ref[...] = encode(squared, bounds[1], 17)


def cube_kernel(
    layer_ref,
    col_ref,
    pattern_ref,
    own_ref,
    other_ref,
    strip_ref,
    out_ref,
    joined,
    turned,
    chunks,
    sems,
    *,
    pair,
    lead,
    bound,
):
    layer = layer_ref[0]
    blocks, half, side = own_ref.shape
    copies = chunk_copies(other_ref, chunks, sems)
    for copy in copies:
        copy.start()
    rows = pair * side
    width = joined.shape[1]
    lanes = pl.ds(pl.multiple_of(layer * (side - width), 128), width)
    strips = []
    total = jnp.zeros((half, width), F32)
    for n in range(lead):
        strips.append(decode17(strip_ref[n * rows : (n + 1) * rows, lanes]))
        own = jnp.concatenate([own_ref[n * pair + i] for i in range(pair)], axis=1)
        total += jnp.dot(own, strips[n], preferred_element_type=F32)
    for copy in copies:
        copy.wait()
    others = jnp.zeros((half, width), F32)
    for n in range(lead):
        other = jnp.concatenate([chunks[n, i] for i in range(pair)], axis=1)
        others += jnp.dot(other, strips[n], preferred_element_type=F32)
    total = jnp.concatenate([total, others], axis=0)
    for n in range(lead, blocks // pair):
        strip = decode17(strip_ref[n * rows : (n + 1) * rows, lanes])
        both = jnp.concatenate(
            [
                jnp.concatenate([own_ref[n * pair + i], chunks[n, i]], axis=0)
                for i in range(pair)
            ],
            axis=1,
        )
        total += jnp.dot(both, strip, preferred_element_type=F32)
    joined[pl.ds(pl.multiple_of(layer * half, half), half), :] = total[:half]
    joined[pl.ds(pl.multiple_of((1 - layer) * half, half), half), :] = total[half:]
    col = col_ref[0]
    square = decode17(strip_ref[pl.ds(pl.multiple_of(col * side, side), side), lanes])
    turned[...] = ((3.0 * square.astype(F32) - 2.0 * joined[...]) * (bound * STEP)).T
    result = turned[pl.ds(pl.multiple_of(layer * (width - half), 8), half), :]
    tiles = half // TILE
    mask = masked_rows(pattern_ref, layer * tiles, tiles, side, False)
    out_ref[...] = (result * mask).astype(BF16)


def shards(density, product_pattern):
    layers = lax.axis_size("layer")
    layer = jnp.reshape(lax.axis_index("layer"), (1,))
    col = jnp.reshape(lax.axis_index("col"), (1,))
    rows, cols = lax.axis_size("row"), lax.axis_size("col")
    side = density.shape[0]
    half = side // layers
    width = -(-half // 128) * 128
    pair = 2
    bound = 2.0
    square_bound = 2.0 ** (2 + (side * rows - 1).bit_length() - 1)
    vmem = pl.BlockSpec(memory_space=pltpu.VMEM)
    smem = pl.BlockSpec(memory_space=pltpu.SMEM)
    hbm = pl.BlockSpec(memory_space=pltpu.HBM)
    claims = [pltpu.CompilerParams(vmem_limit_bytes=n << 20) for n in (56, 50, 24)]
    copies, code = pl.pallas_call(
        functools.partial(start_kernel, bound=bound),
        out_shape=(
            pltpu.HBM((rows, half, side), BF16),
            pltpu.VMEM((half, side), jnp.int16),
        ),
        in_specs=[smem, hbm],
        out_specs=(hbm, vmem),
        scratch_shapes=[
            pltpu.VMEM((side, width), BF16),
            pltpu.VMEM((width, side), F32),
            pltpu.VMEM((half, side), BF16),
            pltpu.SemaphoreType.DMA((rows,)),
            pltpu.SemaphoreType.DMA,
        ],
        compiler_params=claims[0],
    )(layer, density)
    right = lax.all_to_all(copies, "row", 0, 0)
    left = lax.all_gather(code, ("col", "layer"), tiled=True)
    right, left = lax.optimization_barrier((right, left))
    code = pl.pallas_call(
        functools.partial(square_kernel, pair=pair, group=2, bounds=(bound, square_bound)),
        out_shape=jax.ShapeDtypeStruct((half, side), jnp.int16),
        in_specs=[smem, smem, vmem, hbm],
        out_specs=vmem,
        scratch_shapes=[
            pltpu.VMEM((cols // pair, pair * side, side), jnp.int16),
            pltpu.SemaphoreType.DMA((cols // pair,)),
        ],
        compiler_params=claims[1],
    )(layer, product_pattern, right, left)
    other = lax.ppermute(right, "layer", [(i, layers - 1 - i) for i in range(layers)])
    strip = lax.all_gather(code, ("col", "layer"), tiled=True)
    return pl.pallas_call(
        functools.partial(cube_kernel, pair=pair, lead=4, bound=square_bound),
        out_shape=jax.ShapeDtypeStruct((half, side), BF16),
        in_specs=[smem, smem, smem, vmem, hbm, vmem],
        out_specs=vmem,
        scratch_shapes=[
            pltpu.VMEM((side, width), F32),
            pltpu.VMEM((width, side), F32),
            pltpu.VMEM((rows // pair, pair, half, side), BF16),
            pltpu.SemaphoreType.DMA((rows // pair,)),
        ],
        compiler_params=claims[2],
    )(layer, col, product_pattern, right, other, strip)


def solution(mesh):
    placed = (P("row", "col"), P("row", "col"))
    return jax.shard_map(
        shards, mesh=mesh, in_specs=placed, out_specs=P(("row", "layer"), "col"), check_vma=False
    )
```

```python
import functools

import jax
import jax.numpy as jnp
from jax import lax
from jax.experimental import pallas as pl
from jax.experimental.pallas import tpu as pltpu
from jax.sharding import PartitionSpec as P

TILE = 64
STEP = 2.0**-15
F32, BF16 = jnp.float32, jnp.bfloat16


def encode(values, bound, power):
    size = jnp.abs(values) * (1.0 / bound)
    level = jnp.exp(jnp.log(jnp.maximum(size, 1e-37)) * (1.0 / power)) * (1.0 / STEP) + 0.5
    level = jnp.where(size > 1e-36, jnp.minimum(level, 32767.0), 0.0)
    return jnp.where(values < 0, -level, level).astype(jnp.int32).astype(jnp.int16)


def decode7(codes):
    q = codes.astype(jnp.int32).astype(F32)
    q2 = q * q
    q4 = q2 * q2
    return ((q4 * q2) * q).astype(BF16)


def decode17(codes):
    q = codes.astype(jnp.int32).astype(F32)
    s2 = (q * q) * (STEP * STEP)
    s4 = s2 * s2
    s8 = s4 * s4
    return ((s8 * s8) * q).astype(BF16)


def chunk_copies(source, chunks, sems):
    rows = chunks.shape[1]
    return [
        pltpu.make_async_copy(source.at[pl.ds(n * rows, rows)], chunks.at[n], sems.at[n])
        for n in range(chunks.shape[0])
    ]


def masked_rows(pattern_ref, first, count, columns, transposed):
    lane_tile = lax.broadcasted_iota(jnp.int32, (TILE, columns), 1) // TILE
    out = []
    for i in range(count):
        row = jnp.zeros((TILE, columns), F32)
        for j in range(columns // TILE):
            here = pattern_ref[j, first + i] if transposed else pattern_ref[first + i, j]
            row = jnp.where(lane_tile == j, here.astype(F32), row)
        out.append(row)
    return jnp.concatenate(out, axis=0)


def start_kernel(
    layer_ref, block_ref, copies_ref, code_ref, fetched, turned, mine, sems, fetch_sem, *, bound
):
    half, side = code_ref.shape
    width = fetched.shape[1]
    lanes = pl.ds(pl.multiple_of(layer_ref[0] * (side - width), 128), width)
    fetch = pltpu.make_async_copy(block_ref.at[:, lanes], fetched, fetch_sem)
    fetch.start()
    fetch.wait()
    turned[...] = fetched[...].astype(F32).T
    values = turned[pl.ds(pl.multiple_of(layer_ref[0] * (width - half), 8), half), :]
    mine[...] = values.astype(BF16)
    copies = [
        pltpu.make_async_copy(mine, copies_ref.at[n], sems.at[n])
        for n in range(copies_ref.shape[0])
    ]
    for copy in copies:
        copy.start()
    code_ref[...] = encode(values, bound, 7)
    for copy in copies:
        copy.wait()


def square_kernel(
    layer_ref, pattern_ref, right_ref, left_ref, code_ref, chunks, sems, *, pair, group, bounds
):
    half, side = code_ref.shape
    copies = chunk_copies(left_ref, chunks, sems)
    for copy in copies:
        copy.start()
    tiles = half // TILE
    mask = masked_rows(pattern_ref, layer_ref[0] * tiles, tiles, side, True)
    total = jnp.zeros((half, side), F32)
    for n in range(len(copies)):
        if n % group == 0:
            for copy in copies[n : n + group]:
                copy.wait()
        right = jnp.concatenate([right_ref[n * pair + i] for i in range(pair)], axis=1)
        total += jnp.dot(right, decode7(chunks[n]), preferred_element_type=F32)
    squared = (total * (bounds[0] * STEP**7) * mask).astype(BF16).astype(F32)
    code_ref[...] = encode(squared, bounds[1], 17)


def cube_kernel(
    layer_ref,
    col_ref,
    pattern_ref,
    own_ref,
    other_ref,
    strip_ref,
    out_ref,
    joined,
    turned,
    chunks,
    sems,
    *,
    pair,
    lead,
    bound,
):
    layer = layer_ref[0]
    blocks, half, side = own_ref.shape
    copies = chunk_copies(other_ref, chunks, sems)
    for copy in copies:
        copy.start()
    rows = pair * side
    width = joined.shape[1]
    lanes = pl.ds(pl.multiple_of(layer * (side - width), 128), width)
    tiles = half // TILE
    mask = masked_rows(pattern_ref, layer * tiles, tiles, side, False)
    col = col_ref[0]
    square = decode17(strip_ref[pl.ds(pl.multiple_of(col * side, side), side), lanes])
    strips = []
    total = jnp.zeros((half, width), F32)
    for n in range(lead):
        strips.append(decode17(strip_ref[n * rows : (n + 1) * rows, lanes]))
        own = jnp.concatenate([own_ref[n * pair + i] for i in range(pair)], axis=1)
        total += jnp.dot(own, strips[n], preferred_element_type=F32)
    for copy in copies:
        copy.wait()
    others = jnp.zeros((half, width), F32)
    for n in range(lead):
        other = jnp.concatenate([chunks[n, i] for i in range(pair)], axis=1)
        others += jnp.dot(other, strips[n], preferred_element_type=F32)
    total = jnp.concatenate([total, others], axis=0)
    for n in range(lead, blocks // pair):
        strip = decode17(strip_ref[n * rows : (n + 1) * rows, lanes])
        both = jnp.concatenate(
            [
                jnp.concatenate([own_ref[n * pair + i], chunks[n, i]], axis=0)
                for i in range(pair)
            ],
            axis=1,
        )
        total += jnp.dot(both, strip, preferred_element_type=F32)
    joined[pl.ds(pl.multiple_of(layer * half, half), half), :] = total[:half]
    joined[pl.ds(pl.multiple_of((1 - layer) * half, half), half), :] = total[half:]
    turned[...] = ((3.0 * square.astype(F32) - 2.0 * joined[...]) * (bound * STEP)).T
    result = turned[pl.ds(pl.multiple_of(layer * (width - half), 8), half), :]
    out_ref[...] = (result * mask).astype(BF16)


def shards(density, product_pattern):
    layers = lax.axis_size("layer")
    layer = jnp.reshape(lax.axis_index("layer"), (1,))
    col = jnp.reshape(lax.axis_index("col"), (1,))
    rows, cols = lax.axis_size("row"), lax.axis_size("col")
    side = density.shape[0]
    half = side // layers
    width = -(-half // 128) * 128
    pair = 2
    bound = 2.0
    square_bound = 2.0 ** (2 + (side * rows - 1).bit_length() - 1)
    vmem = pl.BlockSpec(memory_space=pltpu.VMEM)
    smem = pl.BlockSpec(memory_space=pltpu.SMEM)
    hbm = pl.BlockSpec(memory_space=pltpu.HBM)
    claims = [pltpu.CompilerParams(vmem_limit_bytes=n << 20) for n in (56, 50, 24)]
    copies, code = pl.pallas_call(
        functools.partial(start_kernel, bound=bound),
        out_shape=(
            pltpu.HBM((rows, half, side), BF16),
            pltpu.VMEM((half, side), jnp.int16),
        ),
        in_specs=[smem, hbm],
        out_specs=(hbm, vmem),
        scratch_shapes=[
            pltpu.VMEM((side, width), BF16),
            pltpu.VMEM((width, side), F32),
            pltpu.VMEM((half, side), BF16),
            pltpu.SemaphoreType.DMA((rows,)),
            pltpu.SemaphoreType.DMA,
        ],
        compiler_params=claims[0],
    )(layer, density)
    right = lax.all_to_all(copies, "row", 0, 0)
    left = lax.all_gather(code, ("col", "layer"), tiled=True)
    right, left = lax.optimization_barrier((right, left))
    code = pl.pallas_call(
        functools.partial(square_kernel, pair=pair, group=2, bounds=(bound, square_bound)),
        out_shape=jax.ShapeDtypeStruct((half, side), jnp.int16),
        in_specs=[smem, smem, vmem, hbm],
        out_specs=vmem,
        scratch_shapes=[
            pltpu.VMEM((cols // pair, pair * side, side), jnp.int16),
            pltpu.SemaphoreType.DMA((cols // pair,)),
        ],
        compiler_params=claims[1],
    )(layer, product_pattern, right, left)
    other = lax.ppermute(right, "layer", [(i, layers - 1 - i) for i in range(layers)])
    strip = lax.all_gather(code, ("col", "layer"), tiled=True)
    return pl.pallas_call(
        functools.partial(cube_kernel, pair=pair, lead=2, bound=square_bound),
        out_shape=jax.ShapeDtypeStruct((half, side), BF16),
        in_specs=[smem, smem, smem, vmem, hbm, vmem],
        out_specs=vmem,
        scratch_shapes=[
            pltpu.VMEM((side, width), F32),
            pltpu.VMEM((width, side), F32),
            pltpu.VMEM((rows // pair, pair, half, side), BF16),
            pltpu.SemaphoreType.DMA((rows // pair,)),
        ],
        compiler_params=claims[2],
    )(layer, col, product_pattern, right, other, strip)


def solution(mesh):
    placed = (P("row", "col"), P("row", "col"))
    return jax.shard_map(
        shards, mesh=mesh, in_specs=placed, out_specs=P(("row", "layer"), "col"), check_vma=False
    )
```
